32 devices in a mesh: groups: 2 (over x), expert: 16 (over z, y, core).
Axes of the slice: x: 2, y: 2, z: 4, core: 2. Of those that a mesh axis runs over, the one named last changes fastest.
Arguments:
- queries: bfloat16 [64, 8192], P(('groups', 'expert')), parts along dimension 0, may hold values from -20 to 20
- kv_cache: bfloat16 [64, 2, 1024, 512], P(('groups', 'expert')), parts along dimension 0, may hold values from -6 to 6
- lengths: int32 [64], P(('groups', 'expert')), parts along dimension 0, may hold values from 2 to 1024, as said below
- moe_input: bfloat16 [2048, 4096], P(('groups', 'expert')), parts along dimension 0, may hold values from -6 to 6
- route_ids: int32 [2048, 8], P(('groups', 'expert')), parts along dimension 0, may hold values from 0 to 15, all different within a row; in each aligned block of 64 rows (0 to 63, 64 to 127, ...) at most 48 rows name the same one
- route_weights: float32 [2048, 8], P(('groups', 'expert')), parts along dimension 0, may hold values from 0.05 to 1
- w_gate_up: bfloat16 [16, 4096, 1536], P('expert'), may hold values from -0.09375 to 0.09375
- w_down: bfloat16 [16, 768, 4096], P('expert'), may hold values from -0.21875 to 0.21875
Outputs:
- attended: bfloat16 [64, 8192], P(('groups', 'expert')), parts along dimension 0
- moe_out: bfloat16 [2048, 4096], P(('groups', 'expert')), parts along dimension 0
The draws below stay inside these ranges and needn't reach their ends.
There are 2 independent parts, one for each index of `groups`. The reference program is written for one: setup_inputs(seed, part) draws one part's arguments, and reference() takes and returns one part's arrays. A program takes and returns all parts, laid end to end along the dimension named above; an argument that names none is the same for every part. Nothing has to cross between parts.
Inputs may be any that keep to these rules, and one draw needn't show every extreme that they name: `route_ids`: in the rows of one device (aligned blocks of 64 rows) no expert is named more than 48 times, a bound that some block reaches; a row names 8 different experts. `lengths`: some request has length exactly 1024.
All inputs are finite; a program needn't handle non-finite values.
Results may differ from the reference program's by a relative error of at most 0.0058.
Values may be sent and summed in bfloat16 or wider, within the bound.
No kernel may reach another device: no remote copies, remote signals or barrier semaphores. Data moves between devices by JAX's collectives and lax.ppermute only.
A program may use at most 128 MiB of HBM per device.

```python
import math
import jax
import jax.numpy as jnp
import numpy as np
from jax import lax

D = 4096
FF = 768
HEADS = 64
KVH = 4
HD = 128
TOP = 8
CTX = 1024
TOK_DEV = 64
EXPERTS = 16
CAP = 48
TOKENS = 1024
REQUESTS = 32
N_EXPERT = 16


def draw_queries(key, part):
    key = jax.random.fold_in(key, 1)
    group_size = HEADS // KVH
    queries_drawn = jax.random.truncated_normal(key, -6.0, 6.0, (REQUESTS, KVH, group_size, HD))
    return queries_drawn.reshape(REQUESTS, HEADS * HD).astype(jnp.bfloat16)


def draw_kv_cache(key, part):
    key = jax.random.fold_in(key, 2)
    cache_shape = (REQUESTS, 2, CTX, KVH * HD)
    cache_drawn = jax.random.truncated_normal(key, -6.0, 6.0, cache_shape)
    return cache_drawn.astype(jnp.bfloat16)


def draw_lengths(key, part):
    key = jax.random.fold_in(key, 3)
    drawn_lengths = jax.random.randint(key, (REQUESTS,), 2, CTX + 1)
    return drawn_lengths.at[0].set(CTX).astype(jnp.int32)


def level_of(stream_key, dims, cuts, low, largest):
    level, own = 1.0, jax.random.fold_in(stream_key, 6)
    for position, blocks in cuts:
        steps = jnp.exp(jax.random.uniform(jax.random.fold_in(own, position), (blocks,), jnp.float32, low / len(cuts), largest / len(cuts)))
        level = level * jnp.repeat(steps, dims[position] // blocks).reshape([-1 if axis == position else 1 for axis in range(len(dims))])
    return level


def assign_block(rng, own, number, rows, count, top, bound, lean):
    order = jax.random.permutation(rng, count)
    heavy_load, usual = portions_of(count, rows * top, bound, lean, True), portions_of(count, rows * top, bound, lean, False)
    places = jnp.arange(count)

    def named(tallies, turn):
        used = int((tallies > 0).sum())
        fixed = max(1, used // 4)
        passed = fixed + (places - fixed + turn * (used - fixed)) % max(1, count - fixed)
        return jnp.zeros((count,), jnp.int32).at[order[jnp.where(places < fixed, places, passed)]].set(jnp.asarray(tallies, jnp.int32))

    tallies = jnp.where(number % 4 == 0, named(heavy_load, number // 4), named(usual, number - number // 4 - 1))
    mixed = jax.random.permutation(jax.random.fold_in(own, 3), count)
    donor, taker = mixed[0:count // 2 * 2:2], mixed[1:count // 2 * 2:2]
    room = jnp.minimum(tallies[donor] - 1, bound - tallies[taker]) // 2
    room = jnp.where((donor == order[0]) | (taker == order[0]) | (tallies[taker] == 0), 0, jnp.maximum(room, 0))
    passed = jax.random.randint(jax.random.fold_in(own, 4), (count // 2,), 0, 1 << 20) % (room + 1)
    tallies = tallies.at[donor].add(-passed).at[taker].add(passed)
    members = jnp.searchsorted(jnp.cumsum(tallies), jnp.arange(rows * top), side="right").astype(jnp.int32)
    listing = members.reshape(top, rows).T
    listing = listing[jax.random.permutation(jax.random.fold_in(own, 1), rows)]
    turn = jax.random.randint(jax.random.fold_in(own, 2), (rows, 1), 0, top)
    return jnp.take_along_axis(listing, (jnp.arange(top)[None, :] + turn) % top, axis=1)


def portions_of(count, total, limit, lean, full):
    loads = [(1 << 20) // math.isqrt(standing ** lean) + 1 for standing in range(1, count + 1)]
    largest = limit if full else min(limit, max(-(-total // count), total * loads[0] // sum(loads)))
    least = 1 if total - largest >= count - 1 else 0
    holding, spare = [largest] + [least] * (count - 1), total - largest - least * (count - 1)
    while spare > 0:
        candidates = [i for i in range(1, count) if holding[i] < largest] or [i for i in range(1, count) if holding[i] < limit]
        pool, remaining = sum([loads[i] for i in candidates]), spare
        for i in candidates:
            extra = min(limit - holding[i], max(1, remaining * loads[i] // pool), spare)
            holding[i] = holding[i] + extra
            spare = spare - extra
    return np.array(holding)


def gaussian(key, shape, scale, bound, cuts=(), kind=jnp.bfloat16):
    factor_of = level_of(key, shape, cuts, -0.22, 0.18) if cuts else 1.0
    array = jax.random.normal(key, shape, jnp.float32) * scale * factor_of
    return jnp.minimum(jnp.maximum(array, -bound), bound).astype(kind)


def setup_inputs(seed: int = 0, part: int = 0) -> dict:
    key_list = jax.random.split(jax.random.key(seed), 9)
    part_splits = jax.random.split(jax.random.fold_in(key_list[8], part), 9)
    queries = draw_queries(jax.random.fold_in(jax.random.fold_in(key_list[8], part), 71), part)
    kv_cache = draw_kv_cache(jax.random.fold_in(jax.random.fold_in(key_list[8], part), 71), part)
    lengths = draw_lengths(jax.random.fold_in(jax.random.fold_in(key_list[8], part), 71), part)
    moe_input = gaussian(part_splits[3], (TOKENS, D), 1.0, 6.0, ((0, 16),))
    route_ids_keys = jax.random.split(jax.random.fold_in(part_splits[4], 1), TOKENS // TOK_DEV)
    route_ids_turns = jax.random.permutation(jax.random.fold_in(part_splits[4], 3), TOKENS // TOK_DEV)
    route_ids = jax.vmap(lambda own, number: assign_block(jax.random.fold_in(part_splits[4], 2), own, number, TOK_DEV, EXPERTS, TOP, CAP, 2))(route_ids_keys, route_ids_turns).reshape((TOKENS, TOP))
    route_weights = jnp.clip(jnp.exp(math.log(1.0) - 2.9957323 * jax.random.uniform(part_splits[5], (TOKENS, TOP), jnp.float32) ** level_of(part_splits[5], (TOKENS, TOP), ((0, 16),), -0.2, 0.2)), 0.05, 1.0)
    w_gate_up = gaussian(key_list[6], (EXPERTS, D, 2 * FF), D ** -0.5, 0.09375, ((0, 16),))
    w_down = gaussian(key_list[7], (EXPERTS, FF, D), FF ** -0.5, 0.21875, ((0, 16),))
    return {"queries": queries, "kv_cache": kv_cache, "lengths": lengths, "moe_input": moe_input, "route_ids": route_ids, "route_weights": route_weights, "w_gate_up": w_gate_up, "w_down": w_down}


def attend_all(queries, kv_cache, lengths):
    requests = queries.shape[0]
    group_size = HEADS // KVH
    query_rows = queries.astype(jnp.float32).reshape(requests, KVH, group_size, HD)
    key_rows = kv_cache[:, 0].astype(jnp.float32).reshape(requests, CTX, KVH, HD)
    value_rows = kv_cache[:, 1].astype(jnp.float32).reshape(requests, CTX, KVH, HD)
    scores = jnp.einsum("rghd,rpgd->rghp", query_rows, key_rows) * (HD ** -0.5)
    visible = jnp.arange(CTX, dtype=jnp.int32)[None, :] < lengths[:, None]
    scores = jnp.where(visible[:, None, None, :], scores, -jnp.inf)
    peak_score = jnp.max(scores, axis=-1, keepdims=True)
    raised = jnp.exp(scores - peak_score)
    weights_low = (raised / jnp.sum(raised, axis=-1, keepdims=True)).astype(jnp.bfloat16)
    mixed_heads = jnp.einsum("rghp,rpgd->rghd", weights_low.astype(jnp.float32), value_rows)
    return mixed_heads.reshape(requests, HEADS * HD).astype(jnp.bfloat16)


def expert_apply(token_rows, gate_up, down_weight):
    projected = jnp.dot(token_rows, gate_up, preferred_element_type=jnp.float32)
    hidden = (jax.nn.silu(projected[:, :FF]) * projected[:, FF:]).astype(jnp.bfloat16)
    return jnp.dot(hidden, down_weight, preferred_element_type=jnp.float32).astype(jnp.bfloat16)


def expert_item(packed):
    return expert_apply(packed[0], packed[1], packed[2])


def reference(queries, kv_cache, lengths, moe_input, route_ids, route_weights, w_gate_up, w_down):
    attended = attend_all(queries, kv_cache, lengths)
    source_count = N_EXPERT
    flat_ids = route_ids.reshape(source_count, TOK_DEV * TOP)
    matches = flat_ids[:, :, None] == jnp.arange(EXPERTS, dtype=jnp.int32)[None, None, :]
    running = jnp.cumsum(matches.astype(jnp.int32), axis=1).astype(jnp.int32) - 1
    slot_index = jnp.sum(jnp.where(matches, running, 0), axis=2).astype(jnp.int32)
    owner_rows = jnp.arange(source_count, dtype=jnp.int32)[:, None]
    destination = ((flat_ids * source_count + owner_rows) * CAP + slot_index).reshape(-1).astype(jnp.int32)
    token_index = (jnp.arange(TOKENS * TOP, dtype=jnp.int32) // TOP).astype(jnp.int32)
    row_table = jnp.full((EXPERTS * source_count * CAP,), TOKENS, jnp.int32).at[destination].set(token_index)
    padded = jnp.concatenate([moe_input, jnp.zeros((1, D), moe_input.dtype)], axis=0)
    buffers = padded[row_table].reshape(EXPERTS, source_count * CAP, D)
    outputs = lax.map(expert_item, (buffers, w_gate_up, w_down))
    picked = outputs.reshape(-1, D)[destination].astype(jnp.float32).reshape(TOKENS, TOP, D)
    share_norm = route_weights / jnp.sum(route_weights, axis=1, keepdims=True)
    moe_out = jnp.sum(share_norm[:, :, None] * picked, axis=1).astype(jnp.bfloat16)
    return attended, moe_out
```

```python
import functools

import jax
import jax.numpy as jnp
from jax import lax
from jax.experimental import pallas as pl
from jax.experimental.pallas import tpu as pltpu
from jax.sharding import PartitionSpec as P

HEADS = 64
KVH = 4
HD = 128
CTX = 1024
LANES = 128
CHUNKS = 2


def attend_kernel(lengths_ref, q_ref, kv_ref, o_ref):
    request = pl.program_id(0)
    length = lengths_ref[request]
    group_size = HEADS // KVH
    visible = lax.broadcasted_iota(jnp.int32, (group_size, CTX), 1) < length
    for g in range(KVH):
        q = q_ref[0, g * group_size : (g + 1) * group_size, :]
        keys = kv_ref[0, 0, :, g * HD : (g + 1) * HD]
        values = kv_ref[0, 1, :, g * HD : (g + 1) * HD]
        scores = lax.dot_general(
            q, keys, (((1,), (1,)), ((), ())), preferred_element_type=jnp.float32
        ) * HD ** (-0.5)
        scores = jnp.where(visible, scores, -jnp.inf)
        raised = jnp.exp(scores - jnp.max(scores, axis=-1, keepdims=True))
        weights = (raised / jnp.sum(raised, axis=-1, keepdims=True)).astype(jnp.bfloat16)
        mixed = jnp.dot(weights, values, preferred_element_type=jnp.float32)
        o_ref[0, g * group_size : (g + 1) * group_size, :] = mixed.astype(jnp.bfloat16)


def attend_local(queries, kv_cache, lengths):
    requests = queries.shape[0]
    grid_spec = pltpu.PrefetchScalarGridSpec(
        num_scalar_prefetch=1,
        grid=(requests,),
        in_specs=[
            pl.BlockSpec((1, HEADS, HD), lambda r, lens: (r, 0, 0)),
            pl.BlockSpec((1, 2, CTX, KVH * HD), lambda r, lens: (r, 0, 0, 0)),
        ],
        out_specs=pl.BlockSpec((1, HEADS, HD), lambda r, lens: (r, 0, 0)),
    )
    out = pl.pallas_call(
        attend_kernel,
        grid_spec=grid_spec,
        out_shape=jax.ShapeDtypeStruct((requests, HEADS, HD), jnp.bfloat16),
        compiler_params=pltpu.CompilerParams(vmem_limit_bytes=16 << 20),
        cost_estimate=pl.CostEstimate(
            flops=requests * 4 * HEADS * CTX * HD,
            bytes_accessed=requests * 4 * CTX * KVH * HD,
            transcendentals=requests * HEADS * CTX,
        ),
        name="attend",
    )(lengths, queries.reshape(requests, HEADS, HD), kv_cache)
    return out.reshape(requests, HEADS * HD)


def expert_kernel(sel_ref, own_ref, sib_ref, gate_ref, up_ref, down_ref, out_own, out_sib, acc):
    j = pl.program_id(0)
    rows = own_ref.shape[0]
    width = down_ref.shape[2]
    x = jnp.concatenate([own_ref[:, :width], sib_ref[:, :width]], axis=0)
    gate = jnp.dot(x, gate_ref[0], preferred_element_type=jnp.float32)
    up = jnp.dot(x, up_ref[0], preferred_element_type=jnp.float32)
    hidden = (jax.nn.silu(gate) * up).astype(jnp.bfloat16)
    part = jnp.dot(hidden, down_ref[0], preferred_element_type=jnp.float32)

    @pl.when(j == 0)
    def _():
        acc[...] = part

    @pl.when((j > 0) & (j < pl.num_programs(0) - 1))
    def _():
        acc[...] += part

    @pl.when(j == pl.num_programs(0) - 1)
    def _():
        total = acc[...] + part
        for ref, out, at in ((own_ref, out_own, 0), (sib_ref, out_sib, rows)):
            coef = jnp.sum(
                ref[:, width:].astype(jnp.float32) * sel_ref[...], axis=1, keepdims=True
            )
            out[...] = (total[at : at + rows] * coef).astype(jnp.bfloat16)


def expert_apply(sel, own, sib, w_gate_up, w_down):
    rows, wide = own.shape
    _, ff, width = w_down.shape
    block = 256
    steps = ff // block
    whole = pl.BlockSpec((rows, wide), lambda j: (0, 0))
    out_spec = pl.BlockSpec((rows, width), lambda j: (0, 0))
    shape = jax.ShapeDtypeStruct((rows, width), jnp.bfloat16)
    return pl.pallas_call(
        expert_kernel,
        grid=(steps,),
        in_specs=[
            pl.BlockSpec((1, LANES), lambda j: (0, 0)),
            whole,
            whole,
            pl.BlockSpec((1, width, block), lambda j: (0, 0, j)),
            pl.BlockSpec((1, width, block), lambda j: (0, 0, j + steps)),
            pl.BlockSpec((1, block, width), lambda j: (0, j, 0)),
        ],
        out_specs=[out_spec, out_spec],
        out_shape=[shape, shape],
        scratch_shapes=[pltpu.VMEM((2 * rows, width), jnp.float32)],
        compiler_params=pltpu.CompilerParams(vmem_limit_bytes=36 << 20),
        cost_estimate=pl.CostEstimate(
            flops=2 * 2 * rows * width * ff * 3,
            bytes_accessed=2 * 3 * width * ff,
            transcendentals=0,
        ),
        name="expert",
    )(sel, own, sib, w_gate_up, w_gate_up, w_down)


def coefficient_columns(route_ids, route_weights, experts):
    share = route_weights / jnp.sum(route_weights, axis=1, keepdims=True)
    names = route_ids[:, :, None] == jnp.arange(experts, dtype=jnp.int32)[None, None, :]
    coef = jnp.sum(jnp.where(names, share[:, :, None], 0.0), axis=1)
    high = lax.reduce_precision(coef, 8, 7)
    middle = lax.reduce_precision(coef - high, 8, 7)
    low = lax.reduce_precision(coef - high - middle, 8, 7)
    parts = jnp.concatenate([high, middle, low], axis=1)
    return jnp.pad(parts, ((0, 0), (0, LANES - 3 * experts))).astype(jnp.bfloat16)


def shards(order, queries, kv_cache, lengths, moe_input, route_ids, route_weights, w_gate_up, w_down):
    experts = lax.axis_size("expert")
    chips = len(order)
    half = chips // 2
    rows = moe_input.shape[0] // CHUNKS

    def ring(step):
        return [
            (2 * order[i] + c, 2 * order[(i + step) % chips] + c)
            for i in range(chips)
            for c in range(2)
        ]

    forward, backward = ring(1), ring(-1)
    swap = [(i, i ^ 1) for i in range(experts)]

    def send(x, pairs):
        return lax.ppermute(x, "expert", pairs)

    me = lax.axis_index("expert")
    lane = lax.broadcasted_iota(jnp.int32, (1, LANES), 1)
    sel = ((lane % experts == me) & (lane < 3 * experts)).astype(jnp.float32)

    wide = jnp.concatenate(
        [moe_input, coefficient_columns(route_ids, route_weights, experts)], axis=1
    )
    fwd = [wide[k * rows : (k + 1) * rows] for k in range(CHUNKS)]
    bwd = list(fwd)
    slots = []
    partial = []

    def compute(own):
        sib = send(own, swap)
        mine, theirs = expert_apply(sel, own, sib, w_gate_up, w_down)
        partial.append((mine, send(theirs, swap)))

    slots.append({("f", k): k for k in range(CHUNKS)})
    last = wide
    for s in range(1, half + 1):
        arrivals = []
        where = {}
        for k in range(CHUNKS):
            if s < half or k == 0:
                fwd[k] = send(fwd[k], forward)
                where["f", k] = len(arrivals)
                arrivals.append(fwd[k])
            if s < half or k == 1:
                bwd[k] = send(bwd[k], backward)
                where["b", k] = len(arrivals)
                arrivals.append(bwd[k])
        compute(last)
        slots.append(where)
        last = jnp.concatenate(arrivals, axis=0)
    compute(last)

    attended = attend_local(queries, kv_cache, lengths)

    def pieces(s, way, k):
        at = slots[s][way, k] * rows
        return [p[at : at + rows].astype(jnp.float32) for p in partial[s]]

    moving = {}
    for s in range(half, 0, -1):
        for k in range(CHUNKS):
            for way, pairs in (("f", backward), ("b", forward)):
                if (way, k) not in slots[s]:
                    continue
                mine, theirs = pieces(s, way, k)
                total = mine + theirs
                if (way, k) in moving:
                    total = total + moving[way, k].astype(jnp.float32)
                moving[way, k] = send(total.astype(jnp.bfloat16), pairs)
    out = []
    for k in range(CHUNKS):
        mine, theirs = pieces(0, "f", k)
        total = mine + theirs
        for way in ("f", "b"):
            total = total + moving[way, k].astype(jnp.float32)
        out.append(total.astype(jnp.bfloat16))
    return attended, jnp.concatenate(out, axis=0)


def solution(mesh):
    chips = mesh.shape["expert"] // 2
    if mesh.shape["groups"] == 2:
        order = list(range(0, chips, 2)) + list(range(chips - 1, 0, -2))
    else:
        order = list(range(chips))
    placed = (
        P(("groups", "expert"), None),
        P(("groups", "expert"), None, None, None),
        P(("groups", "expert")),
        P(("groups", "expert"), None),
        P(("groups", "expert"), None),
        P(("groups", "expert"), None),
        P("expert", None, None),
        P("expert", None, None),
    )
    return jax.shard_map(
        functools.partial(shards, order),
        mesh=mesh,
        in_specs=placed,
        out_specs=(P(("groups", "expert"), None), P(("groups", "expert"), None)),
        check_vma=False,
    )
```

```python
import functools

import jax
import jax.numpy as jnp
from jax import lax
from jax.experimental import pallas as pl
from jax.experimental.pallas import tpu as pltpu
from jax.sharding import PartitionSpec as P

HEADS = 64
KVH = 4
HD = 128
CTX = 1024
LANES = 128
CHUNKS = 2


def attend_kernel(lengths_ref, q_ref, kv_hbm, o_ref, kv, sems):
    requests = q_ref.shape[0]
    copies = [
        pltpu.make_async_copy(kv_hbm.at[r], kv.at[r], sems.at[r]) for r in range(requests)
    ]
    for copy in copies:
        copy.start()
    group_size = HEADS // KVH
    position = lax.broadcasted_iota(jnp.int32, (group_size, CTX), 1)
    for r in range(requests):
        visible = position < lengths_ref[r]
        copies[r].wait()
        for g in range(KVH):
            q = q_ref[r, g * group_size : (g + 1) * group_size, :]
            keys = kv[r, 0, :, g * HD : (g + 1) * HD]
            values = kv[r, 1, :, g * HD : (g + 1) * HD]
            scores = lax.dot_general(
                q, keys, (((1,), (1,)), ((), ())), preferred_element_type=jnp.float32
            ) * HD ** (-0.5)
            scores = jnp.where(visible, scores, -jnp.inf)
            raised = jnp.exp(scores - jnp.max(scores, axis=-1, keepdims=True))
            weights = (raised / jnp.sum(raised, axis=-1, keepdims=True)).astype(jnp.bfloat16)
            mixed = jnp.dot(weights, values, preferred_element_type=jnp.float32)
            o_ref[r, g * group_size : (g + 1) * group_size, :] = mixed.astype(jnp.bfloat16)


def attend_local(queries, kv_cache, lengths):
    requests = queries.shape[0]
    whole = pl.BlockSpec(memory_space=pltpu.VMEM)
    out = pl.pallas_call(
        attend_kernel,
        in_specs=[
            pl.BlockSpec(memory_space=pltpu.SMEM),
            whole,
            pl.BlockSpec(memory_space=pl.ANY),
        ],
        out_specs=whole,
        out_shape=jax.ShapeDtypeStruct((requests, HEADS, HD), jnp.bfloat16),
        scratch_shapes=[
            pltpu.VMEM(kv_cache.shape, kv_cache.dtype),
            pltpu.SemaphoreType.DMA((requests,)),
        ],
        compiler_params=pltpu.CompilerParams(vmem_limit_bytes=6 << 20),
        cost_estimate=pl.CostEstimate(
            flops=requests * 4 * HEADS * CTX * HD,
            bytes_accessed=2 * kv_cache.size,
            transcendentals=requests * HEADS * CTX,
        ),
        name="attend",
    )(
        lengths,
        queries.reshape(requests, HEADS, HD),
        pltpu.with_memory_space_constraint(kv_cache, pltpu.HBM),
    )
    return out.reshape(requests, HEADS * HD)


def expert_kernel(experts, own_ref, sib_ref, in_ref, down_ref, out_own, out_sib, x, hidden):
    rows = own_ref.shape[0]
    _, ff, width = down_ref.shape
    block = 256
    out_block = 1024
    x[:rows, :] = own_ref[:, :width]
    x[rows:, :] = sib_ref[:, :width]
    for n in range(0, ff, block):
        gate = jnp.dot(x[...], in_ref[0, :, n : n + block], preferred_element_type=jnp.float32)
        up = jnp.dot(
            x[...], in_ref[0, :, ff + n : ff + n + block], preferred_element_type=jnp.float32
        )
        hidden[:, n : n + block] = (jax.nn.silu(gate) * up).astype(jnp.bfloat16)
    lane = lax.broadcasted_iota(jnp.int32, (rows, LANES), 1)
    mine = (lax.rem(lane, experts) == lax.axis_index("expert")) & (lane < 3 * experts)
    own_coef, sib_coef = [
        jnp.sum(
            jnp.where(mine, ref[:, width:].astype(jnp.float32), 0.0), axis=1, keepdims=True
        )
        for ref in (own_ref, sib_ref)
    ]
    for n in range(0, width, out_block):
        part = jnp.dot(
            hidden[...], down_ref[0, :, n : n + out_block], preferred_element_type=jnp.float32
        )
        out_own[:, n : n + out_block] = (part[:rows] * own_coef).astype(jnp.bfloat16)
        out_sib[:, n : n + out_block] = (part[rows:] * sib_coef).astype(jnp.bfloat16)


def expert_apply(experts, own, sib, w_gate_up, w_down):
    rows, wide = own.shape
    _, ff, width = w_down.shape
    shape = jax.ShapeDtypeStruct((rows, width), jnp.bfloat16)
    whole = pl.BlockSpec(memory_space=pltpu.VMEM)
    return pl.pallas_call(
        functools.partial(expert_kernel, experts),
        in_specs=[whole] * 4,
        out_specs=[whole] * 2,
        out_shape=[shape, shape],
        scratch_shapes=[
            pltpu.VMEM((2 * rows, width), jnp.bfloat16),
            pltpu.VMEM((2 * rows, ff), jnp.bfloat16),
        ],
        compiler_params=pltpu.CompilerParams(vmem_limit_bytes=6 << 20),
        cost_estimate=pl.CostEstimate(
            flops=2 * 2 * rows * width * ff * 3,
            bytes_accessed=8 * rows * width,
            transcendentals=0,
        ),
        name="expert",
    )(
        own,
        sib,
        *(pltpu.with_memory_space_constraint(x, pltpu.VMEM) for x in (w_gate_up, w_down)),
    )


def prologue_kernel(experts, x_ref, ids_ref, weights_ref, *chunk_refs):
    tokens, width = x_ref.shape
    ids = ids_ref[...].T
    raw = weights_ref[...].T
    top = ids.shape[1]
    rows = tokens // len(chunk_refs)
    lane = lax.broadcasted_iota(jnp.int32, (tokens, LANES), 1)
    named = lax.rem(lane, experts)
    share = raw / jnp.sum(raw, axis=1, keepdims=True)
    coef = jnp.zeros((tokens, LANES), jnp.float32)
    for k in range(top):
        coef = coef + jnp.where(ids[:, k : k + 1] == named, share[:, k : k + 1], 0.0)
    high = coef.astype(jnp.bfloat16).astype(jnp.float32)
    middle = (coef - high).astype(jnp.bfloat16).astype(jnp.float32)
    low = coef - high - middle
    parts = jnp.where(lane < experts, high, jnp.where(lane < 2 * experts, middle, low))
    parts = jnp.where(lane < 3 * experts, parts, 0.0).astype(jnp.bfloat16)
    for k, ref in enumerate(chunk_refs):
        ref[:, :width] = x_ref[k * rows : (k + 1) * rows, :]
        ref[:, width:] = parts[k * rows : (k + 1) * rows, :]


def prologue(moe_input, route_ids, route_weights, experts):
    tokens, width = moe_input.shape
    whole = pl.BlockSpec(memory_space=pltpu.VMEM)
    shapes = [
        jax.ShapeDtypeStruct((n, width + LANES), jnp.bfloat16)
        for n in [tokens // CHUNKS] * CHUNKS
    ]
    return pl.pallas_call(
        functools.partial(prologue_kernel, experts),
        in_specs=[whole] * 3,
        out_specs=[whole] * len(shapes),
        out_shape=shapes,
        compiler_params=pltpu.CompilerParams(vmem_limit_bytes=4 << 20),
        name="prologue",
    )(moe_input, route_ids.T, route_weights.T)


def shards(order, queries, kv_cache, lengths, moe_input, route_ids, route_weights, w_gate_up, w_down):
    experts = lax.axis_size("expert")
    chips = len(order)
    half = chips // 2
    rows = moe_input.shape[0] // CHUNKS

    def ring(step):
        return [
            (2 * order[i] + c, 2 * order[(i + step) % chips] + c)
            for i in range(chips)
            for c in range(2)
        ]

    forward, backward = ring(1), ring(-1)
    swap = [(i, i ^ 1) for i in range(experts)]

    def send(x, pairs):
        return lax.ppermute(x, "expert", pairs)

    first = prologue(moe_input, route_ids, route_weights, experts)
    attended = attend_local(queries, kv_cache, lengths)

    long_pair = (("f", 0), ("b", 1))
    short_pair = (("b", 0), ("f", 1))
    outward = {"f": forward, "b": backward}
    homeward = {"f": backward, "b": forward}

    def tie(anchor, group, values):
        anchor, got = lax.optimization_barrier((anchor, [values[key] for key in group]))
        values.update(zip(group, got))
        return anchor

    def compute(keys, own):
        slots = {key: i * rows for i, key in enumerate(keys)}
        own = jnp.concatenate(own, axis=0)
        mine, theirs = expert_apply(experts, own, send(own, swap), w_gate_up, w_down)
        return [slots, mine, send(theirs, swap)]

    moving = {key: first[key[1]] for key in long_pair + short_pair}
    partial = {}

    def tie_partial(block, index, group, values):
        block[index] = tie(block[index], group, values)

    for s in range(1, half + 2):
        for group in (long_pair, short_pair):
            if group is short_pair and s > half:
                continue
            if s == 2 and group is short_pair:
                attended = tie(attended, group, moving)
            if s > 2:
                tie_partial(partial[s - 2, group], 1, group, moving)
            before = (s - 3, short_pair) if group is long_pair else (s - 2, long_pair)
            if before in partial:
                tie_partial(partial[before], 2, group, moving)
            own = {key: moving[key] for key in group}
            if s < half or (group is long_pair and s == half):
                for key in group:
                    moving[key] = send(moving[key], outward[key[0]])
            if s > 1:
                partial[s - 1, group] = compute(list(own), list(own.values()))
    anchor = partial[half, long_pair]
    anchor[1], first = lax.optimization_barrier((anchor[1], first))
    own_rows = compute(list(range(CHUNKS)), first)

    def local(block, key):
        slots, mine, theirs = block
        span = slice(slots[key], slots[key] + rows)
        return mine[span].astype(jnp.float32) + theirs[span].astype(jnp.float32)

    moving = {}
    last = None
    for s in range(half, 0, -1):
        for group in (short_pair, long_pair) if s < half else (long_pair,):
            if last is not None and group[0] in moving:
                last = tie(last, group, moving)
            if s == 1:
                tie_partial(own_rows, 2, group, moving)
            totals = []
            for key in group:
                total = local(partial[s, group], key)
                if key in moving:
                    total = total + moving[key].astype(jnp.float32)
                totals.append(total.astype(jnp.bfloat16))
            last = totals
            for key, total in zip(group, last):
                moving[key] = send(total, homeward[key[0]])
    out = []
    for k in range(CHUNKS):
        total = local(own_rows, k)
        for way in ("f", "b"):
            total = total + moving[way, k].astype(jnp.float32)
        out.append(total.astype(jnp.bfloat16))
    return attended, jnp.concatenate(out, axis=0)


def solution(mesh):
    chips = mesh.shape["expert"] // 2
    if mesh.shape["groups"] == 2:
        order = list(range(0, chips, 2)) + list(range(chips - 1, 0, -2))
    else:
        order = list(range(chips))
    placed = (
        P(("groups", "expert"), None),
        P(("groups", "expert"), None, None, None),
        P(("groups", "expert")),
        P(("groups", "expert"), None),
        P(("groups", "expert"), None),
        P(("groups", "expert"), None),
        P("expert", None, None),
        P("expert", None, None),
    )
    return jax.shard_map(
        functools.partial(shards, order),
        mesh=mesh,
        in_specs=placed,
        out_specs=(P(("groups", "expert"), None), P(("groups", "expert"), None)),
        check_vma=False,
    )
```

```python
import functools

import jax
import jax.numpy as jnp
from jax import lax
from jax.experimental import pallas as pl
from jax.experimental.pallas import tpu as pltpu
from jax.sharding import PartitionSpec as P

HEADS = 64
KVH = 4
HD = 128
CTX = 1024
LANES = 128
CHUNKS = 2
OPT = {'pair': 'ch', 'swap': 1, 'load_at': (0, 1), 'att_at': (0, 1), 'mine': 2, 'theirs': 3, 'end_mine': 1, 'end_theirs': 1, 'rs': 'B', 'last': 1, 'own_turn': 4, 'att_turn': 6}


def attend_body(request, lengths_ref, q_ref, kv, o_ref):
    length = lengths_ref[request]
    group_size = HEADS // KVH
    visible = lax.broadcasted_iota(jnp.int32, (group_size, CTX), 1) < length
    for g in range(KVH):
        q = q_ref[request, g * group_size : (g + 1) * group_size, :]
        keys = kv[0, :, g * HD : (g + 1) * HD]
        values = kv[1, :, g * HD : (g + 1) * HD]
        scores = lax.dot_general(
            q, keys, (((1,), (1,)), ((), ())), preferred_element_type=jnp.float32
        ) * HD ** (-0.5)
        scores = jnp.where(visible, scores, -jnp.inf)
        raised = jnp.exp(scores - jnp.max(scores, axis=-1, keepdims=True))
        weights = (raised / jnp.sum(raised, axis=-1, keepdims=True)).astype(jnp.bfloat16)
        mixed = jnp.dot(weights, values, preferred_element_type=jnp.float32)
        o_ref[0, g * group_size : (g + 1) * group_size, :] = mixed.astype(jnp.bfloat16)


def attend_kernel(request, lengths_ref, q_ref, kv_hbm, o_ref, kv, sem):
    copy = pltpu.make_async_copy(kv_hbm.at[request], kv, sem)
    copy.start()
    copy.wait()
    attend_body(request, lengths_ref, q_ref, kv, o_ref)


def attend_load_kernel(
    request, lengths_ref, q_ref, kv_hbm, weight_hbm, o_ref, weight_ref, kv, sem, weight_sem
):
    copy = pltpu.make_async_copy(kv_hbm.at[request], kv, sem)
    copy.start()
    load = pltpu.make_async_copy(weight_hbm, weight_ref, weight_sem)
    load.start()
    copy.wait()
    attend_body(request, lengths_ref, q_ref, kv, o_ref)
    load.wait()


def load_kernel(weight_hbm, weight_ref, sem):
    load = pltpu.make_async_copy(weight_hbm, weight_ref, sem)
    load.start()
    load.wait()


VMEM_WHOLE = pl.BlockSpec(memory_space=pltpu.VMEM)
ANYWHERE = pl.BlockSpec(memory_space=pl.ANY)


def in_hbm(x):
    return pltpu.with_memory_space_constraint(x, pltpu.HBM)


def load(weight):
    return pl.pallas_call(
        load_kernel,
        in_specs=[ANYWHERE],
        out_specs=VMEM_WHOLE,
        out_shape=pltpu.VMEM(weight.shape, weight.dtype),
        scratch_shapes=[pltpu.SemaphoreType.DMA],
        compiler_params=pltpu.CompilerParams(vmem_limit_bytes=1 << 20),
        cost_estimate=pl.CostEstimate(
            flops=0, bytes_accessed=2 * weight.size, transcendentals=0
        ),
        name="load",
    )(in_hbm(weight))


def attend(request, queries, kv_cache, lengths, *weight):
    kernel = attend_load_kernel if weight else attend_kernel
    return pl.pallas_call(
        functools.partial(kernel, request),
        in_specs=[pl.BlockSpec(memory_space=pltpu.SMEM), VMEM_WHOLE, ANYWHERE]
        + [ANYWHERE] * len(weight),
        out_specs=[VMEM_WHOLE] * (1 + len(weight)),
        out_shape=[jax.ShapeDtypeStruct((1, HEADS, HD), jnp.bfloat16)]
        + [pltpu.VMEM(w.shape, w.dtype) for w in weight],
        scratch_shapes=[pltpu.VMEM(kv_cache.shape[1:], kv_cache.dtype)]
        + [pltpu.SemaphoreType.DMA] * (1 + len(weight)),
        compiler_params=pltpu.CompilerParams(vmem_limit_bytes=6 << 20),
        cost_estimate=pl.CostEstimate(
            flops=4 * HEADS * CTX * HD,
            bytes_accessed=4 * CTX * KVH * HD + 2 * sum(w.size for w in weight),
            transcendentals=HEADS * CTX,
        ),
        name="attend",
    )(lengths, queries, in_hbm(kv_cache), *(in_hbm(w) for w in weight))


def expert_kernel(experts, own_ref, sib_ref, in_ref, down_ref, out_own, out_sib, x, hidden):
    rows = own_ref.shape[0]
    _, ff, width = down_ref.shape
    block = 256
    out_block = 1024
    x[:rows, :] = own_ref[:, :width]
    x[rows:, :] = sib_ref[:, :width]
    for n in range(0, ff, block):
        gate = jnp.dot(x[...], in_ref[0, :, n : n + block], preferred_element_type=jnp.float32)
        up = jnp.dot(
            x[...], in_ref[0, :, ff + n : ff + n + block], preferred_element_type=jnp.float32
        )
        hidden[:, n : n + block] = (jax.nn.silu(gate) * up).astype(jnp.bfloat16)
    lane = lax.broadcasted_iota(jnp.int32, (rows, LANES), 1)
    mine = (lax.rem(lane, experts) == lax.axis_index("expert")) & (lane < 3 * experts)
    own_coef, sib_coef = [
        jnp.sum(
            jnp.where(mine, ref[:, width:].astype(jnp.float32), 0.0), axis=1, keepdims=True
        )
        for ref in (own_ref, sib_ref)
    ]
    for n in range(0, width, out_block):
        part = jnp.dot(
            hidden[...], down_ref[0, :, n : n + out_block], preferred_element_type=jnp.float32
        )
        out_own[:, n : n + out_block] = (part[:rows] * own_coef).astype(jnp.bfloat16)
        out_sib[:, n : n + out_block] = (part[rows:] * sib_coef).astype(jnp.bfloat16)


def expert_apply(experts, own, sib, w_gate_up, w_down):
    rows, wide = own.shape
    _, ff, width = w_down.shape
    shape = jax.ShapeDtypeStruct((rows, width), jnp.bfloat16)
    whole = pl.BlockSpec(memory_space=pltpu.VMEM)
    return pl.pallas_call(
        functools.partial(expert_kernel, experts),
        in_specs=[whole] * 4,
        out_specs=[whole] * 2,
        out_shape=[shape, shape],
        scratch_shapes=[
            pltpu.VMEM((2 * rows, width), jnp.bfloat16),
            pltpu.VMEM((2 * rows, ff), jnp.bfloat16),
        ],
        compiler_params=pltpu.CompilerParams(vmem_limit_bytes=6 << 20),
        cost_estimate=pl.CostEstimate(
            flops=2 * 2 * rows * width * ff * 3,
            bytes_accessed=8 * rows * width,
            transcendentals=0,
        ),
        name="expert",
    )(
        own,
        sib,
        *(pltpu.with_memory_space_constraint(x, pltpu.VMEM) for x in (w_gate_up, w_down)),
    )


def prologue_kernel(experts, x_hbm, ids_hbm, weights_hbm, *refs):
    chunk_refs = refs[:CHUNKS]
    ids_ref, weights_ref, sems = refs[CHUNKS:]
    tokens, width = x_hbm.shape
    top = ids_hbm.shape[0]
    rows = tokens // CHUNKS
    small = [
        pltpu.make_async_copy(ids_hbm, ids_ref, sems.at[0]),
        pltpu.make_async_copy(weights_hbm, weights_ref, sems.at[1]),
    ]
    large = [
        pltpu.make_async_copy(
            x_hbm.at[pl.ds(k * rows, rows)], ref.at[:, pl.ds(0, width)], sems.at[2 + k]
        )
        for k, ref in enumerate(chunk_refs)
    ]
    for copy in small + large:
        copy.start()
    for copy in small:
        copy.wait()
    ids = ids_ref[...].T
    raw = weights_ref[...].T
    lane = lax.broadcasted_iota(jnp.int32, (tokens, LANES), 1)
    named = lax.rem(lane, experts)
    share = raw / jnp.sum(raw, axis=1, keepdims=True)
    coef = jnp.zeros((tokens, LANES), jnp.float32)
    for k in range(top):
        coef = coef + jnp.where(ids[:, k : k + 1] == named, share[:, k : k + 1], 0.0)
    high = coef.astype(jnp.bfloat16).astype(jnp.float32)
    middle = (coef - high).astype(jnp.bfloat16).astype(jnp.float32)
    low = coef - high - middle
    parts = jnp.where(lane < experts, high, jnp.where(lane < 2 * experts, middle, low))
    parts = jnp.where(lane < 3 * experts, parts, 0.0).astype(jnp.bfloat16)
    for k, ref in enumerate(chunk_refs):
        ref[:, width:] = parts[k * rows : (k + 1) * rows, :]
    for copy in large:
        copy.wait()


def prologue(moe_input, route_ids, route_weights, experts):
    tokens, width = moe_input.shape
    top = route_ids.shape[1]
    return pl.pallas_call(
        functools.partial(prologue_kernel, experts),
        in_specs=[ANYWHERE] * 3,
        out_specs=[VMEM_WHOLE] * CHUNKS,
        out_shape=[
            jax.ShapeDtypeStruct((tokens // CHUNKS, width + LANES), jnp.bfloat16)
        ] * CHUNKS,
        scratch_shapes=[
            pltpu.VMEM((top, tokens), jnp.int32),
            pltpu.VMEM((top, tokens), jnp.float32),
            pltpu.SemaphoreType.DMA((2 + CHUNKS,)),
        ],
        compiler_params=pltpu.CompilerParams(vmem_limit_bytes=4 << 20),
        name="prologue",
    )(in_hbm(moe_input), in_hbm(route_ids.T), in_hbm(route_weights.T))


def shards(order, queries, kv_cache, lengths, moe_input, route_ids, route_weights, w_gate_up, w_down):
    experts = lax.axis_size("expert")
    chips = len(order)
    half = chips // 2
    rows = moe_input.shape[0] // CHUNKS

    def ring(step):
        return [
            (2 * order[i] + c, 2 * order[(i + step) % chips] + c)
            for i in range(chips)
            for c in range(2)
        ]

    forward, backward = ring(1), ring(-1)
    swap = [(i, i ^ 1) for i in range(experts)]

    def send(x, pairs):
        return lax.ppermute(x, "expert", pairs)

    first = prologue(moe_input, route_ids, route_weights, experts)
    requests = queries.shape[0]
    heads = queries.reshape(requests, HEADS, HD)
    gate_up = load(w_gate_up)
    begun, down = attend(0, heads, kv_cache, lengths, w_down)

    long_pair = (("f", 0), ("b", 1))
    short_pair = (("b", 0), ("f", 1))
    outward = {"f": forward, "b": backward}
    homeward = {"f": backward, "b": forward}

    def tie(anchor, group, values):
        anchor, got = lax.optimization_barrier((anchor, [values[key] for key in group]))
        values.update(zip(group, got))
        return anchor

    def compute(keys, own):
        slots = {key: i * rows for i, key in enumerate(keys)}
        own = jnp.concatenate(own, axis=0)
        mine, theirs = expert_apply(experts, own, send(own, swap), gate_up, down)
        return [slots, mine, send(theirs, swap)]

    def tie_partial(block, index, group, values):
        if group:
            block[index] = tie(block[index], group, values)

    longs = long_pair
    if OPT["pair"] == "ls":
        groups = (long_pair, short_pair)
    else:
        groups = ((("f", 0), ("b", 0)), (("f", 1), ("b", 1)))
    if OPT["swap"]:
        groups = groups[::-1]
    moving = {key: first[key[1]] for key in long_pair + short_pair}
    partial = {}
    done = []
    for s in range(1, half + 1):
        for turn, group in enumerate(groups):
            if s == 2 and turn in OPT["load_at"]:
                gate_up = tie(gate_up, group, moving)
            if s == 2 and turn in OPT["att_at"]:
                begun = tie(begun, group, moving)
            if s > 2 and OPT["mine"] and len(done) >= OPT["mine"]:
                tie_partial(done[-OPT["mine"]], 1, group, moving)
            if OPT["theirs"] and len(done) >= OPT["theirs"]:
                tie_partial(done[-OPT["theirs"]], 2, group, moving)
            own = {key: moving[key] for key in group}
            for key in group:
                if s < half or key in longs:
                    moving[key] = send(moving[key], outward[key[0]])
            if s > 1:
                done.append(compute(list(own), list(own.values())))
                for key in own:
                    partial[s - 1, key] = done[-1]
    own = {key: moving[key] for key in longs}
    if OPT["end_mine"]:
        tie_partial(done[-OPT["end_mine"]], 1, longs, own)
    if OPT["end_theirs"]:
        tie_partial(done[-OPT["end_theirs"]], 2, longs, own)
    done.append(compute(list(own), list(own.values())))
    for key in own:
        partial[half, key] = done[-1]
    done[-1][1], first = lax.optimization_barrier((done[-1][1], first))
    own_rows = compute(list(range(CHUNKS)), first)

    def local(block, key):
        slots, mine, theirs = block
        span = slice(slots[key], slots[key] + rows)
        return mine[span].astype(jnp.float32) + theirs[span].astype(jnp.float32)

    if OPT["rs"] == "A":
        order = [(half, long_pair)]
        for s in range(half - 1, 0, -1):
            order += [(s, short_pair), (s, long_pair)]
    else:
        order = [(half - 1, short_pair), (half, long_pair)]
        for s in range(half - 2, 0, -1):
            order += [(s, short_pair), (s + 1, long_pair)]
        order.append((1, long_pair))
    rest = list(range(1, requests))
    attended = [begun]
    moving = {}
    last = None
    for turn, (s, group) in enumerate(order):
        if OPT["last"] and last is not None and group[0] in moving:
            last = tie(last, group, moving)
        if turn == OPT["own_turn"]:
            tie_partial(own_rows, 1, group, moving)
            own_rows[1], heads = lax.optimization_barrier((own_rows[1], heads))
        if turn >= OPT["att_turn"] and rest:
            attended += attend(rest.pop(0), heads, kv_cache, lengths)
            attended[-1] = tie(attended[-1], group, moving)
        if turn == len(order) - 2:
            tie_partial(own_rows, 2, group, moving)
        totals = []
        for key in group:
            total = local(partial[s, key], key)
            if key in moving:
                total = total + moving[key].astype(jnp.float32)
            totals.append(total.astype(jnp.bfloat16))
        last = totals
        for key, total in zip(group, last):
            moving[key] = send(total, homeward[key[0]])
    attended += [attend(r, heads, kv_cache, lengths)[0] for r in rest]
    attended = jnp.concatenate(attended, axis=0).reshape(requests, HEADS * HD)
    out = []
    for k in range(CHUNKS):
        total = local(own_rows, k)
        for way in ("f", "b"):
            total = total + moving[way, k].astype(jnp.float32)
        out.append(total.astype(jnp.bfloat16))
    return attended, jnp.concatenate(out, axis=0)


def solution(mesh):
    chips = mesh.shape["expert"] // 2
    if mesh.shape["groups"] == 2:
        order = list(range(0, chips, 2)) + list(range(chips - 1, 0, -2))
    else:
        order = list(range(chips))
    placed = (
        P(("groups", "expert"), None),
        P(("groups", "expert"), None, None, None),
        P(("groups", "expert")),
        P(("groups", "expert"), None),
        P(("groups", "expert"), None),
        P(("groups", "expert"), None),
        P("expert", None, None),
        P("expert", None, None),
    )
    return jax.shard_map(
        functools.partial(shards, order),
        mesh=mesh,
        in_specs=placed,
        out_specs=(P(("groups", "expert"), None), P(("groups", "expert"), None)),
        check_vma=False,
    )
```

```python
import functools

import jax
import jax.numpy as jnp
from jax import lax
from jax.experimental import pallas as pl
from jax.experimental.pallas import tpu as pltpu
from jax.sharding import PartitionSpec as P

HEADS = 64
KVH = 4
HD = 128
CTX = 1024
LANES = 128
CHUNKS = 2
OPT = {'pair': 'ch', 'swap': 0, 'load_at': [0], 'att_at': [0, 1], 'ties': [[0, 3, 0], [0, 3, 0], [2, 3, 0], [2, 3, 0], [2, 3, 0], [2, 3, 0]], 'end_mine': 1, 'end_theirs': 0, 'rs': 'SLSLLSL', 'last': [1, 1, 1, 1, 1, 1, 1, 1], 'own_turn': 3, 'att_turn': [6], 'chain': [0, 2, 0, 0, 0, 1, 0, 0], 'early': 'down', 'own_ag': 9, 'att_ag': [], 'kv': 'msa', 'merge': 0}


def attend_body(request, lengths_ref, q_ref, kv, o_ref):
    length = lengths_ref[request]
    group_size = HEADS // KVH
    visible = lax.broadcasted_iota(jnp.int32, (group_size, CTX), 1) < length
    for g in range(KVH):
        q = q_ref[request, g * group_size : (g + 1) * group_size, :]
        keys = kv[0, :, g * HD : (g + 1) * HD]
        values = kv[1, :, g * HD : (g + 1) * HD]
        scores = lax.dot_general(
            q, keys, (((1,), (1,)), ((), ())), preferred_element_type=jnp.float32
        ) * HD ** (-0.5)
        scores = jnp.where(visible, scores, -jnp.inf)
        raised = jnp.exp(scores - jnp.max(scores, axis=-1, keepdims=True))
        weights = (raised / jnp.sum(raised, axis=-1, keepdims=True)).astype(jnp.bfloat16)
        mixed = jnp.dot(weights, values, preferred_element_type=jnp.float32)
        o_ref[0, g * group_size : (g + 1) * group_size, :] = mixed.astype(jnp.bfloat16)


def attend_kernel(request, lengths_ref, q_ref, kv_ref, o_ref):
    attend_body(request, lengths_ref, q_ref, kv_ref.at[request], o_ref)


def load_kernel(count, *refs):
    sems = refs[-1]
    copies = [
        pltpu.make_async_copy(refs[i], refs[count + i], sems.at[i]) for i in range(count)
    ]
    for copy in copies:
        copy.start()
    for copy in copies:
        copy.wait()


VMEM_WHOLE = pl.BlockSpec(memory_space=pltpu.VMEM)
ANYWHERE = pl.BlockSpec(memory_space=pl.ANY)


def in_hbm(x):
    return pltpu.with_memory_space_constraint(x, pltpu.HBM)


def load(*arrays):
    return pl.pallas_call(
        functools.partial(load_kernel, len(arrays)),
        in_specs=[ANYWHERE] * len(arrays),
        out_specs=[VMEM_WHOLE] * len(arrays),
        out_shape=[pltpu.VMEM(x.shape, x.dtype) for x in arrays],
        scratch_shapes=[pltpu.SemaphoreType.DMA((len(arrays),))],
        compiler_params=pltpu.CompilerParams(vmem_limit_bytes=1 << 20),
        cost_estimate=pl.CostEstimate(
            flops=0, bytes_accessed=2 * sum(x.size for x in arrays), transcendentals=0
        ),
        name="load",
    )(*(in_hbm(x) for x in arrays))


def attend(request, queries, kv_cache, lengths):
    return pl.pallas_call(
        functools.partial(attend_kernel, request),
        in_specs=[pl.BlockSpec(memory_space=pltpu.SMEM), VMEM_WHOLE, VMEM_WHOLE],
        out_specs=VMEM_WHOLE,
        out_shape=jax.ShapeDtypeStruct((1, HEADS, HD), jnp.bfloat16),
        compiler_params=pltpu.CompilerParams(vmem_limit_bytes=2 << 20),
        cost_estimate=pl.CostEstimate(
            flops=4 * HEADS * CTX * HD,
            bytes_accessed=4 * CTX * KVH * HD,
            transcendentals=HEADS * CTX,
        ),
        name="attend",
    )(lengths, queries, kv_cache)


def expert_kernel(experts, own_ref, sib_ref, in_ref, down_ref, out_own, out_sib, x, hidden):
    rows = own_ref.shape[0]
    _, ff, width = down_ref.shape
    block = 256
    out_block = 1024
    x[:rows, :] = own_ref[:, :width]
    x[rows:, :] = sib_ref[:, :width]
    for n in range(0, ff, block):
        gate = jnp.dot(x[...], in_ref[0, :, n : n + block], preferred_element_type=jnp.float32)
        up = jnp.dot(
            x[...], in_ref[0, :, ff + n : ff + n + block], preferred_element_type=jnp.float32
        )
        hidden[:, n : n + block] = (jax.nn.silu(gate) * up).astype(jnp.bfloat16)
    lane = lax.broadcasted_iota(jnp.int32, (rows, LANES), 1)
    mine = (lax.rem(lane, experts) == lax.axis_index("expert")) & (lane < 3 * experts)
    own_coef, sib_coef = [
        jnp.sum(
            jnp.where(mine, ref[:, width:].astype(jnp.float32), 0.0), axis=1, keepdims=True
        )
        for ref in (own_ref, sib_ref)
    ]
    for n in range(0, width, out_block):
        part = jnp.dot(
            hidden[...], down_ref[0, :, n : n + out_block], preferred_element_type=jnp.float32
        )
        out_own[:, n : n + out_block] = (part[:rows] * own_coef).astype(jnp.bfloat16)
        out_sib[:, n : n + out_block] = (part[rows:] * sib_coef).astype(jnp.bfloat16)


def expert_apply(experts, own, sib, w_gate_up, w_down):
    rows, wide = own.shape
    _, ff, width = w_down.shape
    shape = jax.ShapeDtypeStruct((rows, width), jnp.bfloat16)
    whole = pl.BlockSpec(memory_space=pltpu.VMEM)
    return pl.pallas_call(
        functools.partial(expert_kernel, experts),
        in_specs=[whole] * 4,
        out_specs=[whole] * 2,
        out_shape=[shape, shape],
        scratch_shapes=[
            pltpu.VMEM((2 * rows, width), jnp.bfloat16),
            pltpu.VMEM((2 * rows, ff), jnp.bfloat16),
        ],
        compiler_params=pltpu.CompilerParams(vmem_limit_bytes=6 << 20),
        cost_estimate=pl.CostEstimate(
            flops=2 * 2 * rows * width * ff * 3,
            bytes_accessed=8 * rows * width,
            transcendentals=0,
        ),
        name="expert",
    )(
        own,
        sib,
        *(pltpu.with_memory_space_constraint(x, pltpu.VMEM) for x in (w_gate_up, w_down)),
    )


def prologue_kernel(experts, x_hbm, ids_hbm, weights_hbm, *refs):
    chunk_refs = refs[:CHUNKS]
    ids_ref, weights_ref, sems = refs[CHUNKS:]
    tokens, width = x_hbm.shape
    top = ids_hbm.shape[0]
    rows = tokens // CHUNKS
    small = [
        pltpu.make_async_copy(ids_hbm, ids_ref, sems.at[0]),
        pltpu.make_async_copy(weights_hbm, weights_ref, sems.at[1]),
    ]
    large = [
        pltpu.make_async_copy(
            x_hbm.at[pl.ds(k * rows, rows)], ref.at[:, pl.ds(0, width)], sems.at[2 + k]
        )
        for k, ref in enumerate(chunk_refs)
    ]
    for copy in small + large:
        copy.start()
    for copy in small:
        copy.wait()
    ids = ids_ref[...].T
    raw = weights_ref[...].T
    lane = lax.broadcasted_iota(jnp.int32, (tokens, LANES), 1)
    named = lax.rem(lane, experts)
    share = raw / jnp.sum(raw, axis=1, keepdims=True)
    coef = jnp.zeros((tokens, LANES), jnp.float32)
    for k in range(top):
        coef = coef + jnp.where(ids[:, k : k + 1] == named, share[:, k : k + 1], 0.0)
    high = coef.astype(jnp.bfloat16).astype(jnp.float32)
    middle = (coef - high).astype(jnp.bfloat16).astype(jnp.float32)
    low = coef - high - middle
    parts = jnp.where(lane < experts, high, jnp.where(lane < 2 * experts, middle, low))
    parts = jnp.where(lane < 3 * experts, parts, 0.0).astype(jnp.bfloat16)
    for k, ref in enumerate(chunk_refs):
        ref[:, width:] = parts[k * rows : (k + 1) * rows, :]
    for copy in large:
        copy.wait()


def prologue(moe_input, route_ids, route_weights, experts):
    tokens, width = moe_input.shape
    top = route_ids.shape[1]
    return pl.pallas_call(
        functools.partial(prologue_kernel, experts),
        in_specs=[ANYWHERE] * 3,
        out_specs=[VMEM_WHOLE] * CHUNKS,
        out_shape=[
            jax.ShapeDtypeStruct((tokens // CHUNKS, width + LANES), jnp.bfloat16)
        ] * CHUNKS,
        scratch_shapes=[
            pltpu.VMEM((top, tokens), jnp.int32),
            pltpu.VMEM((top, tokens), jnp.float32),
            pltpu.SemaphoreType.DMA((2 + CHUNKS,)),
        ],
        compiler_params=pltpu.CompilerParams(vmem_limit_bytes=4 << 20),
        name="prologue",
    )(in_hbm(moe_input), in_hbm(route_ids.T), in_hbm(route_weights.T))


def shards(order, queries, kv_cache, lengths, moe_input, route_ids, route_weights, w_gate_up, w_down):
    experts = lax.axis_size("expert")
    chips = len(order)
    half = chips // 2
    rows = moe_input.shape[0] // CHUNKS

    def ring(step):
        return [
            (2 * order[i] + c, 2 * order[(i + step) % chips] + c)
            for i in range(chips)
            for c in range(2)
        ]

    forward, backward = ring(1), ring(-1)
    swap = [(i, i ^ 1) for i in range(experts)]

    def send(x, pairs):
        return lax.ppermute(x, "expert", pairs)

    first = prologue(moe_input, route_ids, route_weights, experts)
    requests = queries.shape[0]
    heads = queries.reshape(requests, HEADS, HD)
    rest = list(range(requests))
    attended = []
    down = w_down
    if OPT["kv"] == "load":
        gate_up, kv_cache = load(w_gate_up, kv_cache)
    else:
        (gate_up,) = load(w_gate_up)

    long_pair = (("f", 0), ("b", 1))
    short_pair = (("b", 0), ("f", 1))
    outward = {"f": forward, "b": backward}
    homeward = {"f": backward, "b": forward}

    def tie(anchor, group, values):
        anchor, got = lax.optimization_barrier((anchor, [values[key] for key in group]))
        values.update(zip(group, got))
        return anchor

    def compute(keys, own):
        slots = {key: i * rows for i, key in enumerate(keys)}
        own = jnp.concatenate(own, axis=0)
        sib = send(own, swap)
        link = OPT["chain"][min(len(done), 7)]
        if 0 < link <= len(done):
            last = done[-link]
            last[1], sib = lax.optimization_barrier((last[1], sib))
        mine, theirs = expert_apply(experts, own, sib, gate_up, down)
        return [slots, mine, send(theirs, swap)]

    def tie_partial(block, index, group, values):
        if group:
            block[index] = tie(block[index], group, values)

    longs = long_pair
    if OPT["pair"] == "ls":
        groups = (long_pair, short_pair)
    else:
        groups = ((("f", 0), ("b", 0)), (("f", 1), ("b", 1)))
    if OPT["swap"]:
        groups = groups[::-1]
    moving = {key: first[key[1]] for key in long_pair + short_pair}
    def tie_heads(heads, done):
        if done:
            done[-1][1], heads = lax.optimization_barrier((done[-1][1], heads))
        return heads

    partial = {}
    done = []
    own_rows = None
    waiting = {}
    for s in range(1, half + 1):
        for turn, group in enumerate(groups):
            if s == 2 and turn in OPT["load_at"]:
                gate_up = tie(gate_up, group, moving)
            before = dict(moving)
            if s > 1:
                mine, theirs, late = OPT["ties"][min(2 * (s - 2) + turn, 5)]
                if 0 < mine <= len(done):
                    tie_partial(done[-mine], 1, group, moving)
                if 0 < theirs <= len(done):
                    tie_partial(done[-theirs], 2, group, moving)
                if not late:
                    before = dict(moving)
            if s == 2 and turn == OPT["own_ag"]:
                own_rows = compute(list(range(CHUNKS)), first)
                done.append(own_rows)
            if s > 1 and 2 * (s - 2) + turn in OPT["att_ag"] and rest:
                heads = tie_heads(heads, done)
                attended.append(attend(rest.pop(0), heads, kv_cache, lengths))
                attended[-1] = tie(attended[-1], group, moving)
            own = {key: before[key] for key in group}
            for key in group:
                if s < half or key in longs:
                    moving[key] = send(moving[key], outward[key[0]])
            if s == half and OPT["merge"]:
                waiting.update(own)
                if turn == 0:
                    continue
                own = waiting
            if s > 1:
                done.append(compute(list(own), list(own.values())))
                for key in own:
                    partial[s - 1, key] = done[-1]
    own = {key: moving[key] for key in longs}
    if OPT["end_mine"]:
        tie_partial(done[-OPT["end_mine"]], 1, longs, own)
    if OPT["end_theirs"]:
        tie_partial(done[-OPT["end_theirs"]], 2, longs, own)
    done.append(compute(list(own), list(own.values())))
    for key in own:
        partial[half, key] = done[-1]
    if own_rows is None:
        done[-1][1], first = lax.optimization_barrier((done[-1][1], first))
        own_rows = compute(list(range(CHUNKS)), first)

    def local(block, key):
        slots, mine, theirs = block
        span = slice(slots[key], slots[key] + rows)
        return mine[span].astype(jnp.float32) + theirs[span].astype(jnp.float32)

    left = {"S": half - 1, "L": half}
    order = []
    for letter in OPT["rs"]:
        order.append((left[letter], short_pair if letter == "S" else long_pair))
        left[letter] -= 1
    for s in range(left["S"], 0, -1):
        order += [(s, short_pair), (left["L"], long_pair)]
        left["L"] -= 1
    for s in range(left["L"], 0, -1):
        order.append((s, long_pair))
    moving = {}
    last = None
    for turn, (s, group) in enumerate(order):
        if OPT["last"][min(turn, 7)] and last is not None and group[0] in moving:
            last = tie(last, group, moving)
        if turn == OPT["own_turn"]:
            tie_partial(own_rows, 1, group, moving)
            own_rows[1], heads = lax.optimization_barrier((own_rows[1], heads))
        if turn in OPT["att_turn"] and rest:
            attended.append(attend(rest.pop(0), heads, kv_cache, lengths))
            attended[-1] = tie(attended[-1], group, moving)
        if turn == len(order) - 2:
            tie_partial(own_rows, 2, group, moving)
        totals = []
        for key in group:
            total = local(partial[s, key], key)
            if key in moving:
                total = total + moving[key].astype(jnp.float32)
            totals.append(total.astype(jnp.bfloat16))
        last = totals
        for key, total in zip(group, last):
            moving[key] = send(total, homeward[key[0]])
    attended += [attend(r, heads, kv_cache, lengths) for r in rest]
    attended = jnp.concatenate(attended, axis=0).reshape(requests, HEADS * HD)
    out = []
    for k in range(CHUNKS):
        total = local(own_rows, k)
        for way in ("f", "b"):
            total = total + moving[way, k].astype(jnp.float32)
        out.append(total.astype(jnp.bfloat16))
    return attended, jnp.concatenate(out, axis=0)


def solution(mesh):
    chips = mesh.shape["expert"] // 2
    if mesh.shape["groups"] == 2:
        order = list(range(0, chips, 2)) + list(range(chips - 1, 0, -2))
    else:
        order = list(range(chips))
    placed = (
        P(("groups", "expert"), None),
        P(("groups", "expert"), None, None, None),
        P(("groups", "expert")),
        P(("groups", "expert"), None),
        P(("groups", "expert"), None),
        P(("groups", "expert"), None),
        P("expert", None, None),
        P("expert", None, None),
    )
    return jax.shard_map(
        functools.partial(shards, order),
        mesh=mesh,
        in_specs=placed,
        out_specs=(P(("groups", "expert"), None), P(("groups", "expert"), None)),
        check_vma=False,
    )
```

```python
import functools

import jax
import jax.numpy as jnp
from jax import lax
from jax.experimental import pallas as pl
from jax.experimental.pallas import tpu as pltpu
from jax.sharding import PartitionSpec as P

HEADS = 64
KVH = 4
HD = 128
CTX = 1024
LANES = 128
CHUNKS = 2
OPT = {'pair': 'ls', 'swap': 1, 'load_at': [0], 'att_at': [0, 1], 'ties': [[0, 3, 0], [0, 3, 0], [2, 3, 0], [2, 3, 0], [2, 3, 0], [0, 4, 0]], 'end_mine': 1, 'end_theirs': 2, 'rs': 'SSLLLSL', 'last': [1, 1, 0, 1, 1, 1, 1, 1], 'own_turn': 3, 'att_turn': [6], 'chain': [0, 2, 0, 0, 0, 1, 0, 0], 'early': 'down', 'own_ag': 9, 'att_ag': [], 'kv': 'msa', 'merge': 0}


def attend_body(request, lengths_ref, q_ref, kv, o_ref):
    length = lengths_ref[request]
    group_size = HEADS // KVH
    visible = lax.broadcasted_iota(jnp.int32, (group_size, CTX), 1) < length
    for g in range(KVH):
        q = q_ref[request, g * group_size : (g + 1) * group_size, :]
        keys = kv[0, :, g * HD : (g + 1) * HD]
        values = kv[1, :, g * HD : (g + 1) * HD]
        scores = lax.dot_general(
            q, keys, (((1,), (1,)), ((), ())), preferred_element_type=jnp.float32
        ) * HD ** (-0.5)
        scores = jnp.where(visible, scores, -jnp.inf)
        raised = jnp.exp(scores - jnp.max(scores, axis=-1, keepdims=True))
        weights = (raised / jnp.sum(raised, axis=-1, keepdims=True)).astype(jnp.bfloat16)
        mixed = jnp.dot(weights, values, preferred_element_type=jnp.float32)
        o_ref[0, g * group_size : (g + 1) * group_size, :] = mixed.astype(jnp.bfloat16)


def attend_kernel(request, lengths_ref, q_ref, kv_ref, o_ref):
    attend_body(request, lengths_ref, q_ref, kv_ref.at[request], o_ref)


def load_kernel(count, *refs):
    sems = refs[-1]
    copies = [
        pltpu.make_async_copy(refs[i], refs[count + i], sems.at[i]) for i in range(count)
    ]
    for copy in copies:
        copy.start()
    for copy in copies:
        copy.wait()


VMEM_WHOLE = pl.BlockSpec(memory_space=pltpu.VMEM)
ANYWHERE = pl.BlockSpec(memory_space=pl.ANY)


def in_hbm(x):
    return pltpu.with_memory_space_constraint(x, pltpu.HBM)


def load(*arrays):
    return pl.pallas_call(
        functools.partial(load_kernel, len(arrays)),
        in_specs=[ANYWHERE] * len(arrays),
        out_specs=[VMEM_WHOLE] * len(arrays),
        out_shape=[pltpu.VMEM(x.shape, x.dtype) for x in arrays],
        scratch_shapes=[pltpu.SemaphoreType.DMA((len(arrays),))],
        compiler_params=pltpu.CompilerParams(vmem_limit_bytes=1 << 20),
        cost_estimate=pl.CostEstimate(
            flops=0, bytes_accessed=2 * sum(x.size for x in arrays), transcendentals=0
        ),
        name="load",
    )(*(in_hbm(x) for x in arrays))


def attend(request, queries, kv_cache, lengths):
    return pl.pallas_call(
        functools.partial(attend_kernel, request),
        in_specs=[pl.BlockSpec(memory_space=pltpu.SMEM), VMEM_WHOLE, VMEM_WHOLE],
        out_specs=VMEM_WHOLE,
        out_shape=jax.ShapeDtypeStruct((1, HEADS, HD), jnp.bfloat16),
        compiler_params=pltpu.CompilerParams(vmem_limit_bytes=2 << 20),
        cost_estimate=pl.CostEstimate(
            flops=4 * HEADS * CTX * HD,
            bytes_accessed=4 * CTX * KVH * HD,
            transcendentals=HEADS * CTX,
        ),
        name="attend",
    )(lengths, queries, kv_cache)


def expert_kernel(experts, own_ref, sib_ref, in_ref, down_ref, out_own, out_sib, x, hidden):
    rows = own_ref.shape[0]
    _, ff, width = down_ref.shape
    block = 256
    out_block = 1024
    x[:rows, :] = own_ref[:, :width]
    x[rows:, :] = sib_ref[:, :width]
    for n in range(0, ff, block):
        gate = jnp.dot(x[...], in_ref[0, :, n : n + block], preferred_element_type=jnp.float32)
        up = jnp.dot(
            x[...], in_ref[0, :, ff + n : ff + n + block], preferred_element_type=jnp.float32
        )
        hidden[:, n : n + block] = (jax.nn.silu(gate) * up).astype(jnp.bfloat16)
    lane = lax.broadcasted_iota(jnp.int32, (rows, LANES), 1)
    mine = (lax.rem(lane, experts) == lax.axis_index("expert")) & (lane < 3 * experts)
    own_coef, sib_coef = [
        jnp.sum(
            jnp.where(mine, ref[:, width:].astype(jnp.float32), 0.0), axis=1, keepdims=True
        )
        for ref in (own_ref, sib_ref)
    ]
    for n in range(0, width, out_block):
        part = jnp.dot(
            hidden[...], down_ref[0, :, n : n + out_block], preferred_element_type=jnp.float32
        )
        out_own[:, n : n + out_block] = (part[:rows] * own_coef).astype(jnp.bfloat16)
        out_sib[:, n : n + out_block] = (part[rows:] * sib_coef).astype(jnp.bfloat16)


def expert_apply(experts, own, sib, w_gate_up, w_down):
    rows, wide = own.shape
    _, ff, width = w_down.shape
    shape = jax.ShapeDtypeStruct((rows, width), jnp.bfloat16)
    whole = pl.BlockSpec(memory_space=pltpu.VMEM)
    return pl.pallas_call(
        functools.partial(expert_kernel, experts),
        in_specs=[whole] * 4,
        out_specs=[whole] * 2,
        out_shape=[shape, shape],
        scratch_shapes=[
            pltpu.VMEM((2 * rows, width), jnp.bfloat16),
            pltpu.VMEM((2 * rows, ff), jnp.bfloat16),
        ],
        compiler_params=pltpu.CompilerParams(vmem_limit_bytes=6 << 20),
        cost_estimate=pl.CostEstimate(
            flops=2 * 2 * rows * width * ff * 3,
            bytes_accessed=8 * rows * width,
            transcendentals=0,
        ),
        name="expert",
    )(
        own,
        sib,
        *(pltpu.with_memory_space_constraint(x, pltpu.VMEM) for x in (w_gate_up, w_down)),
    )


def prologue_kernel(experts, x_hbm, ids_hbm, weights_hbm, *refs):
    chunk_refs = refs[: 2 * CHUNKS]
    ids_ref, weights_ref, sems = refs[2 * CHUNKS :]
    tokens, width = x_hbm.shape
    top = ids_hbm.shape[0]
    rows = tokens // CHUNKS
    small = [
        pltpu.make_async_copy(ids_hbm, ids_ref, sems.at[0]),
        pltpu.make_async_copy(weights_hbm, weights_ref, sems.at[1]),
    ]
    large = [
        pltpu.make_async_copy(
            x_hbm.at[pl.ds(k % CHUNKS * rows, rows)], ref.at[:, pl.ds(0, width)], sems.at[2 + k]
        )
        for k, ref in enumerate(chunk_refs)
    ]
    for copy in small + large:
        copy.start()
    for copy in small:
        copy.wait()
    ids = ids_ref[...].T
    raw = weights_ref[...].T
    lane = lax.broadcasted_iota(jnp.int32, (tokens, LANES), 1)
    named = lax.rem(lane, experts)
    share = raw / jnp.sum(raw, axis=1, keepdims=True)
    coef = jnp.zeros((tokens, LANES), jnp.float32)
    for k in range(top):
        coef = coef + jnp.where(ids[:, k : k + 1] == named, share[:, k : k + 1], 0.0)
    high = coef.astype(jnp.bfloat16).astype(jnp.float32)
    middle = (coef - high).astype(jnp.bfloat16).astype(jnp.float32)
    low = coef - high - middle
    parts = jnp.where(lane < experts, high, jnp.where(lane < 2 * experts, middle, low))
    parts = jnp.where(lane < 3 * experts, parts, 0.0).astype(jnp.bfloat16)
    for k, ref in enumerate(chunk_refs):
        ref[:, width:] = parts[k % CHUNKS * rows : (k % CHUNKS + 1) * rows, :]
    for copy in large:
        copy.wait()


def prologue(moe_input, route_ids, route_weights, experts):
    tokens, width = moe_input.shape
    top = route_ids.shape[1]
    return pl.pallas_call(
        functools.partial(prologue_kernel, experts),
        in_specs=[ANYWHERE] * 3,
        out_specs=[VMEM_WHOLE] * (2 * CHUNKS),
        out_shape=[
            jax.ShapeDtypeStruct((tokens // CHUNKS, width + LANES), jnp.bfloat16)
        ] * (2 * CHUNKS),
        scratch_shapes=[
            pltpu.VMEM((top, tokens), jnp.int32),
            pltpu.VMEM((top, tokens), jnp.float32),
            pltpu.SemaphoreType.DMA((2 + 2 * CHUNKS,)),
        ],
        compiler_params=pltpu.CompilerParams(vmem_limit_bytes=4 << 20),
        name="prologue",
    )(in_hbm(moe_input), in_hbm(route_ids.T), in_hbm(route_weights.T))


def shards(order, queries, kv_cache, lengths, moe_input, route_ids, route_weights, w_gate_up, w_down):
    experts = lax.axis_size("expert")
    chips = len(order)
    half = chips // 2
    rows = moe_input.shape[0] // CHUNKS

    def ring(step):
        return [
            (2 * order[i] + c, 2 * order[(i + step) % chips] + c)
            for i in range(chips)
            for c in range(2)
        ]

    forward, backward = ring(1), ring(-1)
    swap = [(i, i ^ 1) for i in range(experts)]

    def send(x, pairs):
        return lax.ppermute(x, "expert", pairs)

    first = prologue(moe_input, route_ids, route_weights, experts)
    requests = queries.shape[0]
    heads = queries.reshape(requests, HEADS, HD)
    rest = list(range(requests))
    attended = []
    down = w_down
    if OPT["kv"] == "load":
        gate_up, kv_cache = load(w_gate_up, kv_cache)
    else:
        (gate_up,) = load(w_gate_up)

    long_pair = (("f", 0), ("b", 1))
    short_pair = (("b", 0), ("f", 1))
    outward = {"f": forward, "b": backward}
    homeward = {"f": backward, "b": forward}

    def tie(anchor, group, values):
        anchor, got = lax.optimization_barrier((anchor, [values[key] for key in group]))
        values.update(zip(group, got))
        return anchor

    def compute(keys, own):
        slots = {key: i * rows for i, key in enumerate(keys)}
        own = jnp.concatenate(own, axis=0)
        sib = send(own, swap)
        link = OPT["chain"][min(len(done), 7)]
        if 0 < link <= len(done):
            last = done[-link]
            last[1], sib = lax.optimization_barrier((last[1], sib))
        mine, theirs = expert_apply(experts, own, sib, gate_up, down)
        return [slots, mine, send(theirs, swap)]

    def tie_partial(block, index, group, values):
        if group:
            block[index] = tie(block[index], group, values)

    longs = long_pair
    if OPT["pair"] == "ls":
        groups = (long_pair, short_pair)
    else:
        groups = ((("f", 0), ("b", 0)), (("f", 1), ("b", 1)))
    if OPT["swap"]:
        groups = groups[::-1]
    moving = {key: first[key[1] if key in groups[0] else CHUNKS + key[1]] for key in long_pair + short_pair}
    first = first[:CHUNKS]
    def tie_heads(heads, done):
        if done:
            done[-1][1], heads = lax.optimization_barrier((done[-1][1], heads))
        return heads

    partial = {}
    done = []
    own_rows = None
    waiting = {}
    for s in range(1, half + 1):
        for turn, group in enumerate(groups):
            if s == 2 and turn in OPT["load_at"]:
                gate_up = tie(gate_up, group, moving)
            before = dict(moving)
            if s > 1:
                mine, theirs, late = OPT["ties"][min(2 * (s - 2) + turn, 5)]
                if 0 < mine <= len(done):
                    tie_partial(done[-mine], 1, group, moving)
                if 0 < theirs <= len(done):
                    tie_partial(done[-theirs], 2, group, moving)
                if not late:
                    before = dict(moving)
            if s == 2 and turn == OPT["own_ag"]:
                own_rows = compute(list(range(CHUNKS)), first)
                done.append(own_rows)
            if s > 1 and 2 * (s - 2) + turn in OPT["att_ag"] and rest:
                heads = tie_heads(heads, done)
                attended.append(attend(rest.pop(0), heads, kv_cache, lengths))
                attended[-1] = tie(attended[-1], group, moving)
            own = {key: before[key] for key in group}
            for key in group:
                if s < half or key in longs:
                    moving[key] = send(moving[key], outward[key[0]])
            if s == half and OPT["merge"]:
                waiting.update(own)
                if turn == 0:
                    continue
                own = waiting
            if s > 1:
                done.append(compute(list(own), list(own.values())))
                for key in own:
                    partial[s - 1, key] = done[-1]
    own = {key: moving[key] for key in longs}
    if OPT["end_mine"]:
        tie_partial(done[-OPT["end_mine"]], 1, longs, own)
    if OPT["end_theirs"]:
        tie_partial(done[-OPT["end_theirs"]], 2, longs, own)
    done.append(compute(list(own), list(own.values())))
    for key in own:
        partial[half, key] = done[-1]
    if own_rows is None:
        done[-1][1], first = lax.optimization_barrier((done[-1][1], first))
        own_rows = compute(list(range(CHUNKS)), first)

    def local(block, key):
        slots, mine, theirs = block
        span = slice(slots[key], slots[key] + rows)
        return mine[span].astype(jnp.float32) + theirs[span].astype(jnp.float32)

    left = {"S": half - 1, "L": half}
    order = []
    for letter in OPT["rs"]:
        order.append((left[letter], short_pair if letter == "S" else long_pair))
        left[letter] -= 1
    for s in range(left["S"], 0, -1):
        order += [(s, short_pair), (left["L"], long_pair)]
        left["L"] -= 1
    for s in range(left["L"], 0, -1):
        order.append((s, long_pair))
    moving = {}
    last = None
    for turn, (s, group) in enumerate(order):
        if OPT["last"][min(turn, 7)] and last is not None and group[0] in moving:
            last = tie(last, group, moving)
        if turn == OPT["own_turn"]:
            tie_partial(own_rows, 1, group, moving)
            own_rows[1], heads = lax.optimization_barrier((own_rows[1], heads))
        if turn in OPT["att_turn"] and rest:
            attended.append(attend(rest.pop(0), heads, kv_cache, lengths))
            attended[-1] = tie(attended[-1], group, moving)
        if turn == len(order) - 2:
            tie_partial(own_rows, 2, group, moving)
        totals = []
        for key in group:
            total = local(partial[s, key], key)
            if key in moving:
                total = total + moving[key].astype(jnp.float32)
            totals.append(total.astype(jnp.bfloat16))
        last = totals
        for key, total in zip(group, last):
            moving[key] = send(total, homeward[key[0]])
    attended += [attend(r, heads, kv_cache, lengths) for r in rest]
    attended = jnp.concatenate(attended, axis=0).reshape(requests, HEADS * HD)
    out = []
    for k in range(CHUNKS):
        total = local(own_rows, k)
        for way in ("f", "b"):
            total = total + moving[way, k].astype(jnp.float32)
        out.append(total.astype(jnp.bfloat16))
    return attended, jnp.concatenate(out, axis=0)


def solution(mesh):
    chips = mesh.shape["expert"] // 2
    if mesh.shape["groups"] == 2:
        order = list(range(0, chips, 2)) + list(range(chips - 1, 0, -2))
    else:
        order = list(range(chips))
    placed = (
        P(("groups", "expert"), None),
        P(("groups", "expert"), None, None, None),
        P(("groups", "expert")),
        P(("groups", "expert"), None),
        P(("groups", "expert"), None),
        P(("groups", "expert"), None),
        P("expert", None, None),
        P("expert", None, None),
    )
    return jax.shard_map(
        functools.partial(shards, order),
        mesh=mesh,
        in_specs=placed,
        out_specs=(P(("groups", "expert"), None), P(("groups", "expert"), None)),
        check_vma=False,
    )
```
